128 devices in a mesh: aa: 16 (over x, z), ba: 8 (over y, core).
Axes of the slice: x: 4, y: 4, z: 4, core: 2. Of those that a mesh axis runs over, the one named last changes fastest.
Arguments:
- tokens: bfloat16 [2048, 3072], P('aa'), may hold values from -6 to 6
- cotangent: bfloat16 [2048, 3072], P('aa'), may hold values from -6 to 6
- route_scale: float32 [2048, 4], P('aa'), may hold values from 0.05 to 1
- expert_index: int32 [2048, 4], P('aa'), may hold values from 0 to 15, all different within a row; in each aligned block of 128 rows (0 to 127, 128 to 255, ...) at most 48 rows name the same one
- gate_matrix: bfloat16 [16, 3072, 5376], P('aa', None, 'ba'), may hold values from -0.15625 to 0.15625
- up_matrix: bfloat16 [16, 3072, 5376], P('aa', None, 'ba'), may hold values from -0.15625 to 0.15625
- down_matrix: bfloat16 [16, 5376, 3072], P('aa', 'ba'), may hold values from -0.078125 to 0.078125
Outputs:
- token_grad: bfloat16 [2048, 3072], P('aa', 'ba')
- gate_grad: bfloat16 [16, 3072, 5376], P('aa', None, 'ba')
- up_grad: bfloat16 [16, 3072, 5376], P('aa', None, 'ba')
- down_grad: bfloat16 [16, 5376, 3072], P('aa', 'ba')
The draws below stay inside these ranges and needn't reach their ends.
Inputs may be any that keep to these rules, and one draw needn't show every extreme that they name: `expert_index`: each token names 4 different experts. Within each aligned block of 128 rows (the tokens of one index of aa) no expert is named more than 48 times, a bound that some block reaches.
All inputs are finite; a program needn't handle non-finite values.
Results may differ from the reference program's by a relative error of at most 0.02.
Values may be sent and summed in bfloat16 or wider, within the bound.
A program may use at most 192 MiB of HBM per device.

```python
import math
import jax
import jax.numpy as jnp
import numpy as np
from jax import lax

D = 3072
FF = 5376
TOP = 4
TOK_DEV = 128
EXPERTS = 16
TOKENS = 2048
CAP = 48
SLOTS = 768
HID_DEV = 672
N_AA = 16
N_BA = 8


def spiked(entries, own_key, source, target, parts, factor):
    owner, partner = [(jnp.arange(entries.shape[axis_at]) // (entries.shape[axis_at] // parts)).reshape([-1 if axis == axis_at else 1 for axis in range(entries.ndim)]) for axis_at in (source, target)]
    chosen = jax.random.permutation(own_key, parts)[partner]
    strong = (owner == chosen) | (owner == (partner + parts // 2) % parts)
    return jnp.where(strong, factor * entries, entries)


def level_of(stream_key, extent, shards, least, largest):
    def one(dim, parts):
        steps = jax.random.uniform(jax.random.fold_in(jax.random.fold_in(stream_key, 6), dim), (parts,), jnp.float32, least / len(shards), largest / len(shards))
        return jnp.repeat(jnp.exp(steps), extent[dim] // parts).reshape((-1,) + (1,) * (len(extent) - dim - 1))

    level = one(*shards[0])
    for cut in shards[1:]:
        level = level * one(*cut)
    return level


def deal_out(rng, own, number, rows, amount, top, limit, skew):
    order = jax.random.permutation(rng, amount)
    crowded, common = portions_of(amount, rows * top, limit, skew, True), portions_of(amount, rows * top, limit, skew, False)
    places = jnp.arange(amount)

    def named(lengths, offset_by):
        used = int((lengths > 0).sum())
        fixed = max(1, used // 4)
        passed = fixed + (places - fixed + offset_by * (used - fixed)) % max(1, amount - fixed)
        return jnp.zeros((amount,), jnp.int32).at[order[jnp.where(places < fixed, places, passed)]].set(jnp.asarray(lengths, jnp.int32))

    lengths = jnp.where(number % 4 == 0, named(crowded, number // 4), named(common, number - number // 4 - 1))
    mixed = jax.random.permutation(jax.random.fold_in(own, 3), amount)
    donor, receiver = mixed[0:amount // 2 * 2:2], mixed[1:amount // 2 * 2:2]
    room = jnp.minimum(lengths[donor] - 1, limit - lengths[receiver]) // 2
    room = jnp.where((donor == order[0]) | (receiver == order[0]) | (lengths[receiver] == 0), 0, jnp.maximum(room, 0))
    passed = jax.random.randint(jax.random.fold_in(own, 4), (amount // 2,), 0, 1 << 20) % (room + 1)
    lengths = lengths.at[donor].add(-passed).at[receiver].add(passed)
    members = jnp.searchsorted(jnp.cumsum(lengths), jnp.arange(rows * top), side="right").astype(jnp.int32)
    listing = members.reshape(top, rows).T
    listing = listing[jax.random.permutation(jax.random.fold_in(own, 1), rows)]
    offset_by = jax.random.randint(jax.random.fold_in(own, 2), (rows, 1), 0, top)
    return jnp.take_along_axis(listing, (jnp.arange(top)[None, :] + offset_by) % top, axis=1)


def portions_of(amount, total, reach, lean, full):
    loads = [(1 << 20) // math.isqrt(rank ** lean) + 1 for rank in range(1, amount + 1)]
    largest = reach if full else min(reach, max(-(-total // amount), total * loads[0] // sum(loads)))
    least = 1 if total - largest >= amount - 1 else 0
    holding, rest = [largest] + [least] * (amount - 1), total - largest - least * (amount - 1)
    while rest > 0:
        candidates = [i for i in range(1, amount) if holding[i] < largest] or [i for i in range(1, amount) if holding[i] < reach]
        whole, remaining = sum([loads[i] for i in candidates]), rest
        for i in candidates:
            more = min(reach - holding[i], max(1, remaining * loads[i] // whole), rest)
            holding[i] = holding[i] + more
            rest = rest - more
    return np.array(holding)


def normal_values(stream_key, extent, spread, most, cuts=(), kind=jnp.bfloat16):
    entries = spread * jax.random.normal(stream_key, extent, jnp.float32)
    if cuts:
        entries = entries * level_of(stream_key, extent, cuts, -0.22, 0.18)
    return jnp.clip(entries, -most, most).astype(kind)


def heavy_noise(rng, shape, scale, limit, shards, heavy, held_as=jnp.bfloat16):
    array = scale * jax.random.normal(rng, shape, jnp.float32)
    if shards:
        array = array * level_of(rng, shape, shards, -0.22, 0.18)
    return jnp.clip(spiked(array, jax.random.fold_in(rng, 3), *heavy), -limit, limit).astype(held_as)


def setup_inputs(seed: int = 0) -> dict:
    arg_keys = jax.random.split(jax.random.key(seed), 8)
    tokens = normal_values(arg_keys[0], (TOKENS, D), 1.0, 6.0, ((0, 16),))
    cotangent = normal_values(arg_keys[1], (TOKENS, D), 1.0, 6.0, ((0, 16),))
    route_scale = jnp.clip(jnp.exp(math.log(1.0) - 2.9957323 * jax.random.uniform(arg_keys[2], (TOKENS, TOP), jnp.float32) ** level_of(arg_keys[2], (TOKENS, TOP), ((0, 16),), -0.2, 0.2)), 0.05, 1.0)
    expert_index_keys = jax.random.split(jax.random.fold_in(arg_keys[3], 1), TOKENS // TOK_DEV)
    expert_index_turns = jax.random.permutation(jax.random.fold_in(arg_keys[3], 3), TOKENS // TOK_DEV)
    expert_index = jax.vmap(lambda own, number: deal_out(jax.random.fold_in(arg_keys[3], 2), own, number, TOK_DEV, EXPERTS, TOP, CAP, 2))(expert_index_keys, expert_index_turns).reshape((TOKENS, TOP))
    gate_matrix = heavy_noise(arg_keys[4], (EXPERTS, D, FF), D ** -0.5, 0.15625, ((0, 16), (2, 8)), (2, 1, 8, 2.0))
    up_matrix = heavy_noise(arg_keys[5], (EXPERTS, D, FF), D ** -0.5, 0.15625, ((0, 16), (2, 8)), (2, 1, 8, 2.0))
    down_matrix = normal_values(arg_keys[6], (EXPERTS, FF, D), FF ** -0.5, 0.078125, ((0, 16), (1, 8)))
    return {"tokens": tokens, "cotangent": cotangent, "route_scale": route_scale, "expert_index": expert_index, "gate_matrix": gate_matrix, "up_matrix": up_matrix, "down_matrix": down_matrix}


def slot_layout(expert_index):
    blocks = expert_index.reshape(N_AA, TOK_DEV * TOP)
    labels = jnp.arange(EXPERTS, dtype=jnp.int32)
    onehot = (blocks[:, :, None] == labels[None, None, :]).astype(jnp.int32)
    earlier = jnp.cumsum(onehot, axis=1) - onehot
    ranking = jnp.sum(earlier * onehot, axis=2).astype(jnp.int32)
    source = (jnp.arange(N_AA, dtype=jnp.int32) * CAP)[:, None]
    position = (source + ranking).reshape(TOKENS * TOP).astype(jnp.int32)
    return expert_index.reshape(TOKENS * TOP).astype(jnp.int32), position


def expert_backward(operands):
    slot_rows, slot_scaled, gate_full, up_full, down_full = operands
    pre_gate = jnp.dot(slot_rows, gate_full, preferred_element_type=jnp.float32)
    pre_up = jnp.dot(slot_rows, up_full, preferred_element_type=jnp.float32)
    sigmoid_gate = jax.nn.sigmoid(pre_gate)
    activated = pre_gate * sigmoid_gate
    hidden = (activated * pre_up).astype(jnp.bfloat16)
    back_hidden = jnp.dot(slot_scaled, down_full.T, preferred_element_type=jnp.float32)
    back_gate = (back_hidden * pre_up * sigmoid_gate * (1.0 + pre_gate * (1.0 - sigmoid_gate))).astype(jnp.bfloat16)
    back_up = (back_hidden * activated).astype(jnp.bfloat16)
    grad_down = jnp.dot(hidden.T, slot_scaled, preferred_element_type=jnp.float32).astype(jnp.bfloat16)
    grad_gate = jnp.dot(slot_rows.T, back_gate, preferred_element_type=jnp.float32).astype(jnp.bfloat16)
    grad_up = jnp.dot(slot_rows.T, back_up, preferred_element_type=jnp.float32).astype(jnp.bfloat16)
    kept_gate, kept_up = lax.optimization_barrier((back_gate, back_up))
    blocks_gate = kept_gate.astype(jnp.float32).reshape(SLOTS, N_BA, HID_DEV)
    blocks_up = kept_up.astype(jnp.float32).reshape(SLOTS, N_BA, HID_DEV)
    weights_gate = gate_full.astype(jnp.float32).reshape(D, N_BA, HID_DEV)
    weights_up = up_full.astype(jnp.float32).reshape(D, N_BA, HID_DEV)
    partial_value = jnp.einsum("rbh,dbh->rbd", blocks_gate, weights_gate) + jnp.einsum("rbh,dbh->rbd", blocks_up, weights_up)
    partial_value = lax.optimization_barrier(partial_value.astype(jnp.bfloat16))
    slot_grad = jnp.sum(partial_value.astype(jnp.float32), axis=1).astype(jnp.bfloat16)
    return grad_gate, grad_up, grad_down, slot_grad


def reference(tokens, cotangent, route_scale, expert_index, gate_matrix, up_matrix, down_matrix):
    chosen, position = slot_layout(expert_index)
    numbers = jnp.arange(TOKENS * TOP, dtype=jnp.int32)
    table = jnp.zeros((EXPERTS, SLOTS), jnp.int32).at[chosen, position].set(numbers + 1)
    occupied = table > 0
    which_one = jnp.maximum(table - 1, 0).astype(jnp.int32)
    owner_row = (which_one // TOP).astype(jnp.int32)
    scaled = (route_scale[:, :, None] * cotangent[:, None, :].astype(jnp.float32)).astype(jnp.bfloat16)
    scaled = scaled.reshape(TOKENS * TOP, D)
    zero_value = jnp.zeros((), tokens.dtype)
    rows_all = jnp.where(occupied[:, :, None], tokens[owner_row], zero_value)
    scaled_all = jnp.where(occupied[:, :, None], scaled[which_one], zero_value)
    grad_gate, grad_up, grad_down, slot_grads = lax.map(
        expert_backward, (rows_all, scaled_all, gate_matrix, up_matrix, down_matrix))
    picked = slot_grads[chosen, position].astype(jnp.float32).reshape(TOKENS, TOP, D)
    token_grad = jnp.sum(picked, axis=1).astype(jnp.bfloat16)
    return token_grad, grad_gate, grad_up, grad_down
```

```python
import functools

import jax
import jax.numpy as jnp
from jax import lax
from jax.experimental import pallas as pl
from jax.experimental.pallas import tpu as pltpu
from jax.sharding import PartitionSpec as P

PIECES = 4
GRID = 4
BF16 = jnp.bfloat16
F32 = jnp.float32


def nt(a, b):
    return lax.dot_general(a, b, (((1,), (1,)), ((), ())), preferred_element_type=F32)


def tn(a, b):
    return lax.dot_general(a, b, (((0,), (0,)), ((), ())), preferred_element_type=F32)


def nn(a, b):
    return jnp.dot(a, b, preferred_element_type=F32)


def shifted(me, step, count, sign):
    if count != GRID * GRID:
        return lax.rem(me + sign * step + count, count)
    first = lax.rem(step, GRID)
    second = lax.rem(first + lax.div(step, GRID), GRID)
    row = lax.rem(lax.div(me, GRID) + sign * first + GRID, GRID)
    column = lax.rem(lax.rem(me, GRID) + sign * second + GRID, GRID)
    return row * GRID + column


def exchange_kernel(
    capacity,
    index_ref, scale_ref, tok_hbm, cot_hbm, gate_hbm, up_hbm, down_hbm,
    grad_ref, rows_hbm, act_hbm,
    rows, gate_v, up_v, down_v, piece, stage, select, rank, weight, total, act,
    to_pair, from_pair, to_y, keep, from_y, final, back, last_out, last_in,
    piece_sem, load_sem, xz_s, xz_r, pair_s, pair_r, y_s, y_r, rp_s, rp_r, ry_s, ry_r, rx_s, rx_r,
    last_sem, out_sem,
):
    count = lax.axis_size("aa")
    tokens = tok_hbm.shape[0]
    top = index_ref.shape[1]
    slots = count * capacity
    wide = rows.shape[3]
    width = wide // 2
    group = count // 4 if count >= 4 else 1
    chunks = count // group
    depth = group * capacity
    me = lax.axis_index("aa")
    b = lax.axis_index("ba")
    y, c = lax.div(b, 2), lax.rem(b, 2)
    h = lax.rem(y, 2)
    own = 2 * h + c
    other = 2 * (1 - h) + c
    pair = 2 * y + 1 - c
    after = 2 * lax.rem(y + 1, 4) + c
    before = 2 * lax.rem(y + 3, 4) + c
    across = lax.rem(b + 4, 8)

    barrier = pltpu.get_barrier_semaphore()

    def greet(step, carry):
        pl.semaphore_signal(barrier, inc=1, device_id={"aa": shifted(me, step, count, 1)}, device_id_type=pl.DeviceIdType.MESH)
        return carry

    lax.fori_loop(1, count, greet, 0)
    for neighbour in (pair, after, before, across):
        pl.semaphore_signal(barrier, inc=1, device_id={"ba": neighbour}, device_id_type=pl.DeviceIdType.MESH)

    def piece_load(array, half):
        source = (tok_hbm, cot_hbm)[array]
        start = pl.multiple_of((own + 4 * half) * width, 128)
        return pltpu.make_async_copy(
            source.at[:, pl.ds(start, width)], piece.at[array, :, pl.ds(half * width, width)], piece_sem.at[array, half])

    for array in range(2):
        for half in range(2):
            piece_load(array, half).start()

    def weight_loads(p):
        made = []
        for half in range(2):
            far = (p + 4 * half) * width
            near = half * width
            made.append(pltpu.make_async_copy(gate_hbm.at[0, pl.ds(far, width), :], gate_v.at[p, pl.ds(near, width), :], load_sem.at[0, half, p]))
            made.append(pltpu.make_async_copy(up_hbm.at[0, pl.ds(far, width), :], up_v.at[p, pl.ds(near, width), :], load_sem.at[1, half, p]))
            made.append(pltpu.make_async_copy(down_hbm.at[0, :, pl.ds(far, width)], down_v.at[p, :, pl.ds(near, width)], load_sem.at[2, half, p]))
        return made

    lane = lax.broadcasted_iota(jnp.int32, (tokens, 128), 1)
    packed = jnp.zeros((tokens, 128), F32)
    for k in range(top):
        packed = jnp.where(lane == k, index_ref[:, k : k + 1].astype(F32), packed)
        packed = jnp.where(lane == top + k, scale_ref[:, k : k + 1], packed)
    turned = packed.T
    labels = lax.broadcasted_iota(jnp.int32, (count, tokens), 0).astype(F32)
    chosen = jnp.zeros((count, tokens), F32)
    scales = jnp.zeros((count, tokens), F32)
    for k in range(top):
        hit = labels == turned[k : k + 1, :]
        chosen = jnp.where(hit, 1.0, chosen)
        scales = jnp.where(hit, turned[top + k : top + k + 1, :], scales)
    earlier = lax.broadcasted_iota(jnp.int32, (tokens, tokens), 0) < lax.broadcasted_iota(jnp.int32, (tokens, tokens), 1)
    ranks = nn(chosen.astype(BF16), jnp.where(earlier, 1.0, 0.0).astype(BF16))
    rank[...] = jnp.where(chosen > 0.5, ranks, -1.0)
    weight[...] = scales

    def remote(src, dst, send, recv, **where):
        return pltpu.make_async_remote_copy(
            src_ref=src, dst_ref=dst, send_sem=send, recv_sem=recv, device_id=where, device_id_type=pl.DeviceIdType.MESH)

    def block(o):
        return pl.ds(pl.multiple_of(o * capacity, 16), capacity)

    def chunk(q):
        return pl.ds(pl.multiple_of(q * depth, 16), depth)

    def xz(o):
        return remote(stage.at[o], rows.at[:, own, block(o), :], xz_s.at[o], xz_r.at[o], aa=shifted(me, o, count, 1))

    def to_core(k, o):
        there = rows.at[:, (own, other)[k], block(o), :]
        return remote(there, there, pair_s.at[k, o], pair_r.at[k, o], ba=pair)

    def to_plane(k, o):
        there = rows.at[:, own, block(o), pl.ds(k * width, width)]
        return remote(there, there, y_s.at[k, o], y_r.at[k, o], ba=(after, before)[k])

    def sum_core(k, q):
        return remote(to_pair.at[k, chunk(q), :], from_pair.at[k, chunk(q), :], rp_s.at[k, q], rp_r.at[k, q], ba=pair)

    def sum_plane(k, q):
        half = pl.ds(k * width, width)
        return remote(to_y.at[chunk(q), half], from_y.at[chunk(q), half], ry_s.at[k, q], ry_r.at[k, q], ba=(before, after)[k])

    def home(o):
        return remote(final.at[block(o), :], back.at[block(o), :], rx_s.at[o], rx_r.at[o], aa=shifted(me, o, count, -1))

    def rows_out(q):
        return [pltpu.make_async_copy(rows.at[a, :, chunk(q), :], rows_hbm.at[a, :, chunk(q), :], out_sem.at[a, q]) for a in range(2)]

    def act_out(q):
        return pltpu.make_async_copy(act.at[:, chunk(q), :], act_hbm.at[:, chunk(q), :], out_sem.at[2, q])

    for array in range(2):
        for half in range(2):
            piece_load(array, half).wait()
    for p in range(PIECES):
        for load in weight_loads(p):
            load.start()
    pl.semaphore_wait(barrier, count - 1 + 4)

    def dispatch(step, carry):
        o = lax.rem(step + 1, count)
        expert = shifted(me, o, count, 1)
        hits = rank[pl.ds(expert, 1), :] == lax.broadcasted_iota(jnp.int32, (capacity, tokens), 0).astype(F32)
        picks = jnp.where(hits, 1.0, 0.0)
        scale = jnp.sum(picks * weight[pl.ds(expert, 1), :], axis=1, keepdims=True)
        picks = picks.astype(BF16)
        select[block(o), :] = picks
        stage[o, 0] = nn(picks, piece[0]).astype(BF16)
        stage[o, 1] = (scale * nn(picks, piece[1])).astype(BF16)

        @pl.when(o > 0)
        def _():
            xz(o).start()

        @pl.when(o == 0)
        def _():
            for a in range(2):
                rows[a, own, 0:capacity, :] = stage[0, a]

        return carry

    lax.fori_loop(0, count, dispatch, 0)
    for p in range(PIECES):
        for load in weight_loads(p):
            load.wait()

    lag_c = group + 2
    lag_d = lag_c + 4
    lag_e = lag_d + 6
    steps = lag_e + 4 * (chunks - 1) + 1

    def main(t, carry):
        @pl.when(t < count)
        def _():
            @pl.when(t > 0)
            def _():
                xz(t).wait_recv()

            to_plane(0, t).start()
            to_plane(1, t).start()
            to_core(0, t).start()

        u = t - 1

        @pl.when((u >= 0) & (u < count))
        def _():
            to_plane(0, u).wait_recv()
            to_plane(1, u).wait_recv()
            to_core(1, u).start()

        v = t - lag_c

        @pl.when((v >= 0) & (v < 4 * chunks))
        def _():
            q, j = lax.div(v, 4), lax.rem(v, 4)

            @pl.when(j == 0)
            def _():
                for i in range(group):
                    to_core(0, q * group + i).wait_recv()
                    to_core(1, q * group + i).wait_recv()
                for copy in rows_out(q):
                    copy.start()
                total[...] = jnp.zeros_like(total)

            x = rows[0, j, chunk(q), :]
            total[0] += nn(x, gate_v[j])
            total[1] += nn(x, up_v[j])
            total[2] += nt(rows[1, j, chunk(q), :], down_v[j])

            @pl.when(j == 3)
            def _():
                gate, up, behind = total[0], total[1], total[2]
                sigmoid = jax.nn.sigmoid(gate)
                active = gate * sigmoid
                act[0, chunk(q), :] = (active * up).astype(BF16)
                act[1, chunk(q), :] = (behind * up * sigmoid * (1.0 + gate * (1.0 - sigmoid))).astype(BF16)
                act[2, chunk(q), :] = (behind * active).astype(BF16)
                act_out(q).start()

        w = t - lag_d

        @pl.when((w >= 0) & (w < 4 * chunks))
        def _():
            q, j = lax.div(w, 4), lax.rem(w, 4)
            plane = jnp.where(lax.rem(j, 2) == 0, 1 - h, h)
            core = jnp.where(j < 2, 1 - c, c)
            p = 2 * plane + core
            part = nt(act[1, chunk(q), :], gate_v[p]) + nt(act[2, chunk(q), :], up_v[p])

            @pl.when(j < 2)
            def _():
                to_pair[j, chunk(q), :] = part.astype(BF16)
                sum_core(j, q).start()

            @pl.when(j == 2)
            def _():
                sum_core(0, q).wait_recv()
                to_y[chunk(q), :] = (part + from_pair[0, chunk(q), :].astype(F32)).astype(BF16)
                sum_plane(0, q).start()
                sum_plane(1, q).start()

            @pl.when(j == 3)
            def _():
                sum_core(1, q).wait_recv()
                keep[chunk(q), :] = part + from_pair[1, chunk(q), :].astype(F32)

        z = t - lag_e

        @pl.when((z >= 0) & (lax.rem(z + 4, 4) == 0))
        def _():
            q = lax.div(z, 4)
            sum_plane(0, q).wait_recv()
            sum_plane(1, q).wait_recv()
            final[chunk(q), :] = (keep[chunk(q), :] + from_y[chunk(q), :].astype(F32)).astype(BF16)
            for i in range(group):
                o = q * group + i

                @pl.when(o > 0)
                def _():
                    home(o).start()

                @pl.when(o == 0)
                def _():
                    back[0:capacity, :] = final[0:capacity, :]

        return carry

    lax.fori_loop(0, steps, main, 0)

    def arrive(o, carry):
        home(o).wait_recv()
        return carry

    lax.fori_loop(1, count, arrive, 0)
    merged = tn(select[...], back[...])
    low, high = merged[:, :width], merged[:, width:]
    last_out[...] = jnp.where(y < 2, high, low).astype(BF16)
    swap = remote(last_out, last_in, last_sem.at[0], last_sem.at[1], ba=across)
    swap.start()
    mine = jnp.where(y < 2, low, high)
    swap.wait_recv()
    grad_ref[...] = (mine + last_in[...].astype(F32)).astype(BF16)
    swap.wait_send()

    def settle(o, carry):
        @pl.when(o > 0)
        def _():
            xz(o).wait_send()
            home(o).wait_send()

        for k in range(2):
            to_core(k, o).wait_send()
            to_plane(k, o).wait_send()
        return carry

    lax.fori_loop(0, count, settle, 0)

    def settle_sums(q, carry):
        for k in range(2):
            sum_core(k, q).wait_send()
            sum_plane(k, q).wait_send()
        for copy in rows_out(q):
            copy.wait()
        act_out(q).wait()
        return carry

    lax.fori_loop(0, chunks, settle_sums, 0)


def weight_grads_kernel(rows_ref, scaled_ref, act_ref, gate_ref, up_ref, down_ref):
    x, s = rows_ref[0, 0], scaled_ref[0, 0]
    gate_ref[0] = tn(x, act_ref[1]).astype(BF16)
    up_ref[0] = tn(x, act_ref[2]).astype(BF16)
    down_ref[0] = tn(act_ref[0], s).astype(BF16)


def shards(tokens, cotangent, route_scale, expert_index, gate_matrix, up_matrix, down_matrix):
    rows_here, features = tokens.shape
    top = expert_index.shape[1]
    experts = lax.axis_size("aa")
    capacity = 3 * rows_here * top // (2 * experts)
    slots = experts * capacity
    width = features // 8
    wide = 2 * width
    hidden = gate_matrix.shape[2]
    group = experts // 4 if experts >= 4 else 1
    chunks = experts // group
    depth = group * capacity
    any_, vmem, dma = pl.ANY, pltpu.VMEM, pltpu.SemaphoreType.DMA
    token_grad, slot_rows, acts = pl.pallas_call(
        functools.partial(exchange_kernel, capacity),
        out_shape=(
            jax.ShapeDtypeStruct((rows_here, width), BF16),
            jax.ShapeDtypeStruct((2, PIECES, slots, wide), BF16),
            jax.ShapeDtypeStruct((3, slots, hidden), BF16),
        ),
        in_specs=[pl.BlockSpec(memory_space=vmem)] * 2 + [pl.BlockSpec(memory_space=any_)] * 5,
        out_specs=(pl.BlockSpec(memory_space=vmem), pl.BlockSpec(memory_space=any_), pl.BlockSpec(memory_space=any_)),
        scratch_shapes=[
            vmem((2, PIECES, slots, wide), BF16),
            vmem((PIECES, wide, hidden), BF16),
            vmem((PIECES, wide, hidden), BF16),
            vmem((PIECES, hidden, wide), BF16),
            vmem((2, rows_here, wide), BF16),
            vmem((experts, 2, capacity, wide), BF16),
            vmem((slots, rows_here), BF16),
            vmem((experts, rows_here), F32),
            vmem((experts, rows_here), F32),
            vmem((3, depth, hidden), F32),
            vmem((3, slots, hidden), BF16),
            vmem((2, slots, wide), BF16),
            vmem((2, slots, wide), BF16),
            vmem((slots, wide), BF16),
            vmem((slots, wide), F32),
            vmem((slots, wide), BF16),
            vmem((slots, wide), BF16),
            vmem((slots, wide), BF16),
            vmem((rows_here, width), BF16),
            vmem((rows_here, width), BF16),
            dma((2, 2)),
            dma((3, 2, PIECES)),
            dma((experts,)),
            dma((experts,)),
            dma((2, experts)),
            dma((2, experts)),
            dma((2, experts)),
            dma((2, experts)),
            dma((2, chunks)),
            dma((2, chunks)),
            dma((2, chunks)),
            dma((2, chunks)),
            dma((experts,)),
            dma((experts,)),
            dma((2,)),
            dma((3, chunks)),
        ],
        compiler_params=pltpu.CompilerParams(
            collective_id=0, has_side_effects=True, vmem_limit_bytes=56 * 2**20
        ),
        cost_estimate=pl.CostEstimate(
            flops=10 * slots * features * hidden,
            bytes_accessed=6 * features * hidden + 4 * slots * features,
            transcendentals=slots * hidden,
        ),
    )(expert_index, route_scale, tokens, cotangent, gate_matrix, up_matrix, down_matrix)
    gate_grad, up_grad, down_grad = pl.pallas_call(
        weight_grads_kernel,
        grid=(8,),
        out_shape=(
            jax.ShapeDtypeStruct((1, features, hidden), BF16),
            jax.ShapeDtypeStruct((1, features, hidden), BF16),
            jax.ShapeDtypeStruct((1, hidden, features), BF16),
        ),
        in_specs=[
            pl.BlockSpec((1, 1, slots, width), lambda i: (0, lax.rem(i, 4), 0, lax.div(i, 4))),
            pl.BlockSpec((1, 1, slots, width), lambda i: (1, lax.rem(i, 4), 0, lax.div(i, 4))),
            pl.BlockSpec((3, slots, hidden), lambda i: (0, 0, 0)),
        ],
        out_specs=(
            pl.BlockSpec((1, width, hidden), lambda i: (0, i, 0)),
            pl.BlockSpec((1, width, hidden), lambda i: (0, i, 0)),
            pl.BlockSpec((1, hidden, width), lambda i: (0, 0, i)),
        ),
        compiler_params=pltpu.CompilerParams(vmem_limit_bytes=48 * 2**20),
        cost_estimate=pl.CostEstimate(
            flops=6 * slots * features * hidden,
            bytes_accessed=6 * features * hidden + 4 * slots * features,
            transcendentals=0,
        ),
    )(slot_rows, slot_rows, acts)
    return token_grad, gate_grad, up_grad, down_grad


def solution(mesh):
    in_specs = (
        P("aa", None),
        P("aa", None),
        P("aa", None),
        P("aa", None),
        P("aa", None, "ba"),
        P("aa", None, "ba"),
        P("aa", "ba", None),
    )
    out_specs = (P("aa", "ba"), P("aa", None, "ba"), P("aa", None, "ba"), P("aa", "ba", None))
    return jax.shard_map(shards, mesh=mesh, in_specs=in_specs, out_specs=out_specs, check_vma=False)
```

```python
import functools

import jax
import jax.numpy as jnp
from jax import lax
from jax.experimental import pallas as pl
from jax.experimental.pallas import tpu as pltpu
from jax.sharding import PartitionSpec as P

PIECES = 4
GRID = 4
AHEAD = 5
RELAY_LAG = 3
SLOTS_OUT = 4
CUTS = (3, 8)
BF16 = jnp.bfloat16
F32 = jnp.float32


def nt(a, b):
    return lax.dot_general(a, b, (((1,), (1,)), ((), ())), preferred_element_type=F32)


def tn(a, b):
    return lax.dot_general(a, b, (((0,), (0,)), ((), ())), preferred_element_type=F32)


def nn(a, b):
    return jnp.dot(a, b, preferred_element_type=F32)


def shifted(me, step, count, sign):
    if count != GRID * GRID:
        return lax.rem(me + sign * step + count, count)
    first = lax.rem(step, GRID)
    second = lax.rem(first + lax.div(step, GRID), GRID)
    row = lax.rem(lax.div(me, GRID) + sign * first + GRID, GRID)
    column = lax.rem(lax.rem(me, GRID) + sign * second + GRID, GRID)
    return row * GRID + column


def exchange_kernel(
    capacity,
    index_ref, scale_ref, tok_hbm, cot_hbm, gate_hbm, up_hbm, down_hbm,
    grad_ref, weights_hbm,
    rows, gate_v, up_v, down_v, piece, stage, select, rank, weight, total, act,
    to_pair, from_pair, to_y, keep, from_y, final, back, last_mine, last_out, last_in, turned, made,
    piece_sem, load_sem, xz_s, xz_r, pair_s, pair_r, y_s, y_r, rp_s, rp_r, ry_s, ry_r, rx_s, rx_r,
    last_sem, out_sem,
):
    count = lax.axis_size("aa")
    tokens = tok_hbm.shape[0]
    top = index_ref.shape[0]
    slots = count * capacity
    wide = rows.shape[3]
    width = wide // 2
    group = count // 4 if count >= 4 else 1
    chunks = count // group
    depth = group * capacity
    me = lax.axis_index("aa")
    b = lax.axis_index("ba")
    y, c = lax.div(b, 2), lax.rem(b, 2)
    h = lax.rem(y, 2)
    own = 2 * h + c
    other = 2 * (1 - h) + c
    pair = 2 * y + 1 - c
    after = 2 * lax.rem(y + 1, 4) + c
    before = 2 * lax.rem(y + 3, 4) + c
    across = lax.rem(b + 4, 8)

    barrier = pltpu.get_barrier_semaphore()

    def greet(step, carry):
        pl.semaphore_signal(barrier, inc=1, device_id={"aa": shifted(me, step, count, 1)}, device_id_type=pl.DeviceIdType.MESH)
        return carry

    lax.fori_loop(1, count, greet, 0)
    for neighbour in (pair, after, before, across):
        pl.semaphore_signal(barrier, inc=1, device_id={"ba": neighbour}, device_id_type=pl.DeviceIdType.MESH)

    def piece_load(array, half):
        source = (tok_hbm, cot_hbm)[array]
        start = pl.multiple_of((own + 4 * half) * width, 128)
        return pltpu.make_async_copy(
            source.at[:, pl.ds(start, width)], piece.at[array, :, pl.ds(half * width, width)], piece_sem.at[array, half])

    for array in range(2):
        for half in range(2):
            piece_load(array, half).start()

    def weight_loads(p):
        made = []
        for half in range(2):
            far = (p + 4 * half) * width
            near = half * width
            for k, (source, target) in enumerate(((gate_hbm, gate_v), (up_hbm, up_v), (down_hbm, down_v))):
                made.append(pltpu.make_async_copy(source.at[0, :, pl.ds(far, width)], target.at[p, :, pl.ds(near, width)], load_sem.at[k, half, p]))
        return made

    labels = lax.broadcasted_iota(jnp.int32, (count, tokens), 0)
    chosen = jnp.zeros((count, tokens), F32)
    scales = jnp.zeros((count, tokens), F32)
    for k in range(top):
        hit = labels == index_ref[k : k + 1, :]
        chosen = jnp.where(hit, 1.0, chosen)
        scales = jnp.where(hit, scale_ref[k : k + 1, :], scales)
    earlier = lax.broadcasted_iota(jnp.int32, (tokens, tokens), 0) < lax.broadcasted_iota(jnp.int32, (tokens, tokens), 1)
    ranks = nn(chosen.astype(BF16), jnp.where(earlier, 1.0, 0.0).astype(BF16))
    rank[...] = jnp.where(chosen > 0.5, ranks, -1.0)
    weight[...] = scales

    def remote(src, dst, send, recv, **where):
        return pltpu.make_async_remote_copy(
            src_ref=src, dst_ref=dst, send_sem=send, recv_sem=recv, device_id=where, device_id_type=pl.DeviceIdType.MESH)

    def block(o):
        return pl.ds(pl.multiple_of(o * capacity, 16), capacity)

    def chunk(q):
        return pl.ds(pl.multiple_of(q * depth, 16), depth)

    def xz(o):
        return remote(stage.at[o], rows.at[:, own, block(o), :], xz_s.at[o], xz_r.at[o], aa=shifted(me, o, count, 1))

    def to_core(k, o):
        there = rows.at[:, (own, other)[k], block(o), :]
        return remote(there, there, pair_s.at[k, o], pair_r.at[k, o], ba=pair)

    def to_plane(k, o):
        there = rows.at[:, own, block(o), pl.ds(k * width, width)]
        return remote(there, there, y_s.at[k, o], y_r.at[k, o], ba=(after, before)[k])

    def sum_core(k, q):
        return remote(to_pair.at[k, chunk(q), :], from_pair.at[k, chunk(q), :], rp_s.at[k, q], rp_r.at[k, q], ba=pair)

    def sum_plane(k, q):
        half = pl.ds(k * width, width)
        return remote(to_y.at[chunk(q), half], from_y.at[chunk(q), half], ry_s.at[k, q], ry_r.at[k, q], ba=(before, after)[k])

    def home(o):
        return remote(final.at[block(o), :], back.at[block(o), :], rx_s.at[o], rx_r.at[o], aa=shifted(me, o, count, -1))

    def grad_out(n, half):
        k, p = lax.rem(n, 3), lax.div(n, 3)
        slot = lax.rem(n, SLOTS_OUT)
        there = pl.ds(pl.multiple_of((p + 4 * half) * width, 128), width)
        return pltpu.make_async_copy(
            made.at[slot, :, pl.ds(half * width, width)], weights_hbm.at[k, :, there], out_sem.at[slot, half])

    def grad_step(n, carry):
        k, p = lax.rem(n, 3), lax.div(n, 3)

        @pl.when(n >= SLOTS_OUT)
        def _():
            for half in range(2):
                grad_out(n - SLOTS_OUT, half).wait()

        side = jnp.where(k == 0, 1, 0)
        made[lax.rem(n, SLOTS_OUT)] = nn(turned[k], rows[side, p]).astype(BF16)
        for half in range(2):
            grad_out(n, half).start()
        return carry

    def grads(first, last):
        lax.fori_loop(first, last, grad_step, 0)

    for array in range(2):
        for half in range(2):
            piece_load(array, half).wait()
    for p in range(PIECES):
        for load in weight_loads(p):
            load.start()
    pl.semaphore_wait(barrier, count - 1 + 4)

    def dispatch(step, carry):
        o = lax.rem(step + 1, count)
        expert = shifted(me, o, count, 1)
        hits = rank[pl.ds(expert, 1), :] == lax.broadcasted_iota(jnp.int32, (capacity, tokens), 0).astype(F32)
        picks = jnp.where(hits, 1.0, 0.0)
        scale = jnp.sum(picks * weight[pl.ds(expert, 1), :], axis=1, keepdims=True)
        picks = picks.astype(BF16)
        select[block(o), :] = picks
        stage[o, 0] = nn(picks, piece[0]).astype(BF16)
        stage[o, 1] = (scale * nn(picks, piece[1])).astype(BF16)

        @pl.when((o > 0) & (o < AHEAD))
        def _():
            xz(o).start()

        @pl.when(o == 0)
        def _():
            for a in range(2):
                rows[a, own, 0:capacity, :] = stage[0, a]

        return carry

    lax.fori_loop(0, count, dispatch, 0)
    for p in range(PIECES):
        for load in weight_loads(p):
            load.wait()

    lag_c = group + RELAY_LAG + 1
    lag_d = lag_c + 4
    lag_e = lag_d + 6
    steps = lag_d + 4 * chunks

    def send_home(q):
        sum_plane(0, q).wait_recv()
        sum_plane(1, q).wait_recv()
        final[chunk(q), :] = (keep[chunk(q), :] + from_y[chunk(q), :].astype(F32)).astype(BF16)
        for i in range(group):
            o = q * group + i

            @pl.when(o > 0)
            def _():
                home(o).start()

            @pl.when(o == 0)
            def _():
                back[0:capacity, :] = final[0:capacity, :]

    def main(t, carry):
        @pl.when(t < count)
        def _():
            @pl.when(t > 0)
            def _():
                xz(t).wait_recv()

            to_plane(0, t).start()
            to_plane(1, t).start()
            to_core(0, t).start()

            @pl.when(t + AHEAD < count)
            def _():
                @pl.when(t > 0)
                def _():
                    xz(t).wait_send()

                xz(t + AHEAD).start()

        u = t - RELAY_LAG

        @pl.when((u >= 0) & (u < count))
        def _():
            to_plane(0, u).wait_recv()
            to_plane(1, u).wait_recv()
            to_core(1, u).start()

        v = t - lag_c

        @pl.when((v >= 0) & (v < 4 * chunks))
        def _():
            q, j = lax.div(v, 4), lax.rem(v, 4)

            @pl.when(j == 0)
            def _():
                for i in range(group):
                    to_core(0, q * group + i).wait_recv()
                    to_core(1, q * group + i).wait_recv()
                total[...] = jnp.zeros_like(total)

            x = rows[0, j, chunk(q), :]
            total[0] += nt(x, gate_v[j])
            total[1] += nt(x, up_v[j])
            total[2] += nt(rows[1, j, chunk(q), :], down_v[j])

            @pl.when(j == 3)
            def _():
                gate, up, behind = total[0], total[1], total[2]
                sigmoid = jax.nn.sigmoid(gate)
                active = gate * sigmoid
                act[0, chunk(q), :] = (active * up).astype(BF16)
                act[1, chunk(q), :] = (behind * up * sigmoid * (1.0 + gate * (1.0 - sigmoid))).astype(BF16)
                act[2, chunk(q), :] = (behind * active).astype(BF16)

        w = t - lag_d

        @pl.when((w >= 0) & (w < 4 * chunks))
        def _():
            q, j = lax.div(w, 4), lax.rem(w, 4)
            plane = jnp.where(lax.rem(j, 2) == 0, 1 - h, h)
            core = jnp.where(j < 2, 1 - c, c)
            p = 2 * plane + core
            part = nn(act[1, chunk(q), :], gate_v[p]) + nn(act[2, chunk(q), :], up_v[p])

            @pl.when(j < 2)
            def _():
                to_pair[j, chunk(q), :] = part.astype(BF16)
                sum_core(j, q).start()

            @pl.when(j == 2)
            def _():
                sum_core(0, q).wait_recv()
                to_y[chunk(q), :] = (part + from_pair[0, chunk(q), :].astype(F32)).astype(BF16)
                sum_plane(0, q).start()
                sum_plane(1, q).start()

            @pl.when(j == 3)
            def _():
                sum_core(1, q).wait_recv()
                keep[chunk(q), :] = part + from_pair[1, chunk(q), :].astype(F32)

        z = t - lag_e

        @pl.when((z >= 0) & (z < 4 * (chunks - 1)) & (lax.rem(z + 4, 4) == 0))
        def _():
            send_home(lax.div(z, 4))

        return carry

    lax.fori_loop(0, steps, main, 0)

    def turn(k, carry):
        turned[k] = act[k].T
        return carry

    lax.fori_loop(0, 3, turn, 0)
    grads(0, CUTS[0])
    send_home(chunks - 1)
    grads(CUTS[0], CUTS[1])

    def arrive(o, carry):
        home(o).wait_recv()
        return carry

    lax.fori_loop(1, count, arrive, 0)
    merged = tn(select[...], back[...])
    low, high = merged[:, :width], merged[:, width:]
    last_out[...] = jnp.where(y < 2, high, low).astype(BF16)
    last_mine[...] = jnp.where(y < 2, low, high)
    swap = remote(last_out, last_in, last_sem.at[0], last_sem.at[1], ba=across)
    swap.start()
    grads(CUTS[1], 3 * PIECES)

    def settle(o, carry):
        @pl.when((o > 0) & (o >= count - AHEAD))
        def _():
            xz(o).wait_send()

        @pl.when(o > 0)
        def _():
            home(o).wait_send()

        for k in range(2):
            to_core(k, o).wait_send()
            to_plane(k, o).wait_send()
        return carry

    lax.fori_loop(0, count, settle, 0)

    def settle_sums(q, carry):
        for k in range(2):
            sum_core(k, q).wait_send()
            sum_plane(k, q).wait_send()
        return carry

    lax.fori_loop(0, chunks, settle_sums, 0)
    swap.wait_recv()
    grad_ref[...] = (last_mine[...] + last_in[...].astype(F32)).astype(BF16)
    swap.wait_send()

    def settle_grads(n, carry):
        for half in range(2):
            grad_out(n, half).wait()
        return carry

    lax.fori_loop(3 * PIECES - SLOTS_OUT, 3 * PIECES, settle_grads, 0)


def shards(tokens, cotangent, route_scale, expert_index, gate_matrix, up_matrix, down_matrix):
    rows_here, features = tokens.shape
    top = expert_index.shape[1]
    experts = lax.axis_size("aa")
    capacity = 3 * rows_here * top // (2 * experts)
    slots = experts * capacity
    width = features // 8
    wide = 2 * width
    hidden = gate_matrix.shape[2]
    group = experts // 4 if experts >= 4 else 1
    chunks = experts // group
    depth = group * capacity
    any_, vmem, dma = pl.ANY, pltpu.VMEM, pltpu.SemaphoreType.DMA
    token_grad, weight_grads = pl.pallas_call(
        functools.partial(exchange_kernel, capacity),
        out_shape=(
            jax.ShapeDtypeStruct((rows_here, width), BF16),
            jax.ShapeDtypeStruct((3, hidden, features), BF16),
        ),
        in_specs=[pl.BlockSpec(memory_space=vmem)] * 2 + [pl.BlockSpec(memory_space=any_)] * 5,
        out_specs=(pl.BlockSpec(memory_space=vmem), pl.BlockSpec(memory_space=any_)),
        scratch_shapes=[
            vmem((2, PIECES, slots, wide), BF16),
            vmem((PIECES, hidden, wide), BF16),
            vmem((PIECES, hidden, wide), BF16),
            vmem((PIECES, hidden, wide), BF16),
            vmem((2, rows_here, wide), BF16),
            vmem((experts, 2, capacity, wide), BF16),
            vmem((slots, rows_here), BF16),
            vmem((experts, rows_here), F32),
            vmem((experts, rows_here), F32),
            vmem((3, depth, hidden), F32),
            vmem((3, slots, hidden), BF16),
            vmem((2, slots, wide), BF16),
            vmem((2, slots, wide), BF16),
            vmem((slots, wide), BF16),
            vmem((slots, wide), F32),
            vmem((slots, wide), BF16),
            vmem((slots, wide), BF16),
            vmem((slots, wide), BF16),
            vmem((rows_here, width), F32),
            vmem((rows_here, width), BF16),
            vmem((rows_here, width), BF16),
            vmem((3, hidden, slots), BF16),
            vmem((SLOTS_OUT, hidden, wide), BF16),
            dma((2, 2)),
            dma((3, 2, PIECES)),
            dma((experts,)),
            dma((experts,)),
            dma((2, experts)),
            dma((2, experts)),
            dma((2, experts)),
            dma((2, experts)),
            dma((2, chunks)),
            dma((2, chunks)),
            dma((2, chunks)),
            dma((2, chunks)),
            dma((experts,)),
            dma((experts,)),
            dma((2,)),
            dma((SLOTS_OUT, 2)),
        ],
        compiler_params=pltpu.CompilerParams(
            collective_id=0, has_side_effects=True, vmem_limit_bytes=56 * 2**20
        ),
        cost_estimate=pl.CostEstimate(
            flops=16 * slots * features * hidden,
            bytes_accessed=12 * features * hidden,
            transcendentals=slots * hidden,
        ),
    )(expert_index.T, route_scale.T, tokens, cotangent, jnp.swapaxes(gate_matrix, 1, 2), jnp.swapaxes(up_matrix, 1, 2), down_matrix)
    down_grad, gate_grad, up_grad = weight_grads[0:1], weight_grads[1:2], weight_grads[2:3]
    return token_grad, jnp.swapaxes(gate_grad, 1, 2), jnp.swapaxes(up_grad, 1, 2), down_grad


def solution(mesh):
    in_specs = (
        P("aa", None),
        P("aa", None),
        P("aa", None),
        P("aa", None),
        P("aa", None, "ba"),
        P("aa", None, "ba"),
        P("aa", "ba", None),
    )
    out_specs = (P("aa", "ba"), P("aa", None, "ba"), P("aa", None, "ba"), P("aa", "ba", None))
    return jax.shard_map(shards, mesh=mesh, in_specs=in_specs, out_specs=out_specs, check_vma=False)
```

```python
import functools

import jax
import jax.numpy as jnp
from jax import lax
from jax.experimental import pallas as pl
from jax.experimental.pallas import tpu as pltpu
from jax.sharding import PartitionSpec as P

PIECES = 4
GRID = 4
AHEAD = 6
MOVES = (
    (0, 0), (1, 0), (3, 0), (0, 1), (0, 3), (2, 0), (0, 2), (2, 2),
    (2, 1), (2, 3), (1, 2), (3, 2), (1, 1), (3, 3), (1, 3), (3, 1),
)
RELAY_LAG = 3
SLOTS_OUT = 4
CUTS = (0, 4)
BF16 = jnp.bfloat16
F32 = jnp.float32


def nt(a, b):
    return lax.dot_general(a, b, (((1,), (1,)), ((), ())), preferred_element_type=F32)


def tn(a, b):
    return lax.dot_general(a, b, (((0,), (0,)), ((), ())), preferred_element_type=F32)


def nn(a, b):
    return jnp.dot(a, b, preferred_element_type=F32)


def shifted(me, step, count, sign):
    if count != GRID * GRID:
        return lax.rem(me + sign * step + count, count)
    move = 0
    for k, (dx, dz) in enumerate(MOVES):
        move = jnp.where(step == k, dx * GRID + dz, move)
    first, second = lax.div(move, GRID), lax.rem(move, GRID)
    row = lax.rem(lax.div(me, GRID) + sign * first + GRID, GRID)
    column = lax.rem(lax.rem(me, GRID) + sign * second + GRID, GRID)
    return row * GRID + column


def exchange_kernel(
    capacity,
    index_ref, scale_ref, tok_hbm, cot_hbm, gate_hbm, up_hbm, down_hbm,
    grad_ref, other_ref, weights_hbm, tokens_out_hbm, behind_hbm,
    rows, weights_v, piece, stage, select, rank, weight, total, act,
    to_pair, from_pair, to_y, keep, from_y, final, back, turned, made,
    piece_sem, load_sem, xz_s, xz_r, pair_s, pair_r, y_s, y_r, rp_s, rp_r, ry_s, ry_r, rx_s, rx_r,
    out_sem, pass_sem,
):
    count = lax.axis_size("aa")
    tokens = tok_hbm.shape[0]
    top = index_ref.shape[0]
    slots = count * capacity
    wide = rows.shape[3]
    width = wide // 2
    group = count // 4 if count >= 4 else 1
    chunks = count // group
    depth = group * capacity
    parts = 2 if group % 2 == 0 else 1
    me = lax.axis_index("aa")
    b = lax.axis_index("ba")
    y, c = lax.div(b, 2), lax.rem(b, 2)
    h = lax.rem(y, 2)
    own = 2 * h + c
    other = 2 * (1 - h) + c
    pair = 2 * y + 1 - c
    after = 2 * lax.rem(y + 1, 4) + c
    before = 2 * lax.rem(y + 3, 4) + c
    across = lax.rem(b + 4, 8)

    barrier = pltpu.get_barrier_semaphore()

    def greet(step, carry):
        pl.semaphore_signal(barrier, inc=1, device_id={"aa": shifted(me, step, count, 1)}, device_id_type=pl.DeviceIdType.MESH)
        return carry

    lax.fori_loop(1, count, greet, 0)
    for neighbour in (pair, after, before, across):
        pl.semaphore_signal(barrier, inc=1, device_id={"ba": neighbour}, device_id_type=pl.DeviceIdType.MESH)

    def piece_load(array, half):
        source = (tok_hbm, cot_hbm)[array]
        start = pl.multiple_of((own + 4 * half) * width, 128)
        return pltpu.make_async_copy(
            source.at[:, pl.ds(start, width)], piece.at[array, :, pl.ds(half * width, width)], piece_sem.at[array, half])

    for array in range(2):
        for half in range(2):
            piece_load(array, half).start()

    def weight_loads(p):
        made = []
        for half in range(2):
            far = (p + 4 * half) * width
            near = half * width
            for k, source in enumerate((gate_hbm, up_hbm, down_hbm)):
                made.append(pltpu.make_async_copy(source.at[0, :, pl.ds(far, width)], weights_v.at[k, p, :, pl.ds(near, width)], load_sem.at[k, half, p]))
        return made

    labels = lax.broadcasted_iota(jnp.int32, (count, tokens), 0)
    chosen = jnp.zeros((count, tokens), F32)
    scales = jnp.zeros((count, tokens), F32)
    for k in range(top):
        hit = labels == index_ref[k : k + 1, :]
        chosen = jnp.where(hit, 1.0, chosen)
        scales = jnp.where(hit, scale_ref[k : k + 1, :], scales)
    earlier = lax.broadcasted_iota(jnp.int32, (tokens, tokens), 0) < lax.broadcasted_iota(jnp.int32, (tokens, tokens), 1)
    ranks = nn(chosen.astype(BF16), jnp.where(earlier, 1.0, 0.0).astype(BF16))
    rank[...] = jnp.where(chosen > 0.5, ranks, -1.0)
    weight[...] = scales

    def remote(src, dst, send, recv, **where):
        return pltpu.make_async_remote_copy(
            src_ref=src, dst_ref=dst, send_sem=send, recv_sem=recv, device_id=where, device_id_type=pl.DeviceIdType.MESH)

    def block(o):
        return pl.ds(pl.multiple_of(o * capacity, 16), capacity)

    def chunk(q):
        return pl.ds(pl.multiple_of(q * depth, 16), depth)

    def xz(o):
        return remote(stage.at[o], rows.at[:, own, block(o), :], xz_s.at[o], xz_r.at[o], aa=shifted(me, o, count, 1))

    def to_core(k, o):
        there = rows.at[:, (own, other)[k], block(o), :]
        return remote(there, there, pair_s.at[k, o], pair_r.at[k, o], ba=pair)

    def to_plane(k, o):
        there = rows.at[:, own, block(o), pl.ds(k * width, width)]
        return remote(there, there, y_s.at[k, o], y_r.at[k, o], ba=(after, before)[k])

    def sum_core(k, q):
        return remote(to_pair.at[k, chunk(q), :], from_pair.at[k, chunk(q), :], rp_s.at[k, q], rp_r.at[k, q], ba=pair)

    def portion(i):
        return pl.ds(pl.multiple_of(i * (depth // parts), 16), depth // parts)

    def sum_plane(k, i):
        half = pl.ds(k * width, width)
        return remote(to_y.at[portion(i), half], from_y.at[portion(i), half], ry_s.at[k, i], ry_r.at[k, i], ba=(before, after)[k])

    def home(o):
        return remote(final.at[block(o), :], back.at[block(o), :], rx_s.at[o], rx_r.at[o], aa=shifted(me, o, count, -1))

    def tokens_out(q):
        return pltpu.make_async_copy(rows.at[0, :, chunk(q), :], tokens_out_hbm.at[:, chunk(q), :], pass_sem.at[0, q])

    def behind_out(k):
        return pltpu.make_async_copy(turned.at[k + 1], behind_hbm.at[k], pass_sem.at[1, k])

    def grad_out(n):
        slot = lax.rem(n, SLOTS_OUT)
        return pltpu.make_async_copy(made.at[slot], weights_hbm.at[n], out_sem.at[slot])

    def grad_step(n, carry):
        made[lax.rem(n, SLOTS_OUT)] = nn(turned[0], rows[1, n]).astype(BF16)
        grad_out(n).start()
        return carry

    def grads(first, last):
        lax.fori_loop(first, last, grad_step, 0)

    for array in range(2):
        for half in range(2):
            piece_load(array, half).wait()
    def dispatch(step, carry):
        o = lax.rem(step + 1, count)
        expert = shifted(me, o, count, 1)
        hits = rank[pl.ds(expert, 1), :] == lax.broadcasted_iota(jnp.int32, (capacity, tokens), 0).astype(F32)
        picks = jnp.where(hits, 1.0, 0.0)
        scale = jnp.sum(picks * weight[pl.ds(expert, 1), :], axis=1, keepdims=True)
        picks = picks.astype(BF16)
        select[block(o), :] = picks
        stage[o, 0] = nn(picks, piece[0]).astype(BF16)
        stage[o, 1] = (scale * nn(picks, piece[1])).astype(BF16)

        return carry

    def first_sends(o, carry):
        xz(o).start()
        return carry

    ahead = min(AHEAD, count)
    lax.fori_loop(0, ahead - 1, dispatch, 0)
    pl.semaphore_wait(barrier, count - 1 + 4)
    lax.fori_loop(1, ahead, first_sends, 0)
    lax.fori_loop(ahead - 1, count, dispatch, 0)
    for a in range(2):
        rows[a, own, 0:capacity, :] = stage[0, a]
    for p in range(PIECES):
        for load in weight_loads(p):
            load.start()

    lag_c = group + RELAY_LAG + 1
    lag_d = lag_c + 4
    lag_e = lag_d + 5
    steps = lag_d + 4 * chunks - 2

    def send_home(n):
        sum_plane(0, n).wait_recv()
        sum_plane(1, n).wait_recv()
        final[portion(n), :] = (keep[portion(n), :] + from_y[portion(n), :].astype(F32)).astype(BF16)
        for i in range(group // parts):
            o = n * (group // parts) + i

            @pl.when(o > 0)
            def _():
                home(o).start()

            @pl.when(o == 0)
            def _():
                back[0:capacity, :] = final[0:capacity, :]

    def backward_unit(w, carry):
        q, j = lax.div(w, 4), lax.rem(w, 4)
        plane = jnp.where(lax.rem(j, 2) == 0, 1 - h, h)
        core = jnp.where(j < 2, 1 - c, c)
        p = 2 * plane + core
        part = nn(act[1, chunk(q), :], weights_v[0, p]) + nn(act[2, chunk(q), :], weights_v[1, p])

        @pl.when(j < 2)
        def _():
            to_pair[j, chunk(q), :] = part.astype(BF16)
            sum_core(j, q).start()

        @pl.when(j == 2)
        def _():
            sum_core(0, q).wait_recv()
            to_y[chunk(q), :] = (part + from_pair[0, chunk(q), :].astype(F32)).astype(BF16)
            for i in range(parts):
                sum_plane(0, q * parts + i).start()
                sum_plane(1, q * parts + i).start()

        @pl.when(j == 3)
        def _():
            sum_core(1, q).wait_recv()
            keep[chunk(q), :] = part + from_pair[1, chunk(q), :].astype(F32)
        return carry

    def main(t, carry):
        @pl.when(t < count)
        def _():
            @pl.when(t > 0)
            def _():
                xz(t).wait_recv()

            to_plane(0, t).start()
            to_plane(1, t).start()
            to_core(0, t).start()

            @pl.when(t + AHEAD < count)
            def _():
                @pl.when(t > 0)
                def _():
                    xz(t).wait_send()

                xz(t + AHEAD).start()

        u = t - RELAY_LAG

        @pl.when((u >= 0) & (u < count))
        def _():
            to_plane(0, u).wait_recv()
            to_plane(1, u).wait_recv()
            to_core(1, u).start()

        v = t - lag_c

        @pl.when((v >= 0) & (v < 4 * chunks))
        def _():
            q, j = lax.div(v, 4), lax.rem(v, 4)

            @pl.when(v == 0)
            def _():
                for p in range(PIECES):
                    for load in weight_loads(p):
                        load.wait()

            @pl.when(j == 0)
            def _():
                for i in range(group):
                    to_core(0, q * group + i).wait_recv()
                    to_core(1, q * group + i).wait_recv()
                tokens_out(q).start()

            @pl.when(j < 3)
            def _():
                side = jnp.where(j == 2, 1, 0)
                total[j] = sum(nt(rows[side, p, chunk(q), :], weights_v[j, p]) for p in range(PIECES))

            @pl.when(j == 3)
            def _():
                gate, up, behind = total[0], total[1], total[2]
                sigmoid = jax.nn.sigmoid(gate)
                active = gate * sigmoid
                act[0, chunk(q), :] = (active * up).astype(BF16)
                act[1, chunk(q), :] = (behind * up * sigmoid * (1.0 + gate * (1.0 - sigmoid))).astype(BF16)
                act[2, chunk(q), :] = (behind * active).astype(BF16)

        w = t - lag_d

        @pl.when((w >= 0) & (w < 4 * chunks - 2))
        def _():
            backward_unit(w, 0)

        z = t - lag_e

        @pl.when((z >= 0) & (z < 4 * (chunks - 1)) & (lax.rem(z + 4, 4) == 0))
        def _():
            for i in range(parts):
                send_home(lax.div(z, 4) * parts + i)

        return carry

    lax.fori_loop(0, steps, main, 0)

    turned[0] = act[0].T
    lax.fori_loop(4 * chunks - 2, 4 * chunks, backward_unit, 0)
    for k in range(2):
        turned[k + 1] = act[k + 1].T
        behind_out(k).start()
    grads(0, CUTS[0])
    for i in range(parts):
        send_home(jnp.int32((chunks - 1) * parts + i))
        grads(CUTS[0] + i, CUTS[0] + i + 1)
    grads(CUTS[0] + parts, CUTS[1])

    def arrive(o, carry):
        home(o).wait_recv()
        return carry

    early = (chunks - 1) * depth
    lax.fori_loop(1, count - group, arrive, 0)
    keep[0:tokens, :] = tn(select[0:early, :], back[0:early, :])
    lax.fori_loop(count - group, count, arrive, 0)
    merged = keep[0:tokens, :] + tn(select[early:slots, :], back[early:slots, :])
    low, high = merged[:, :width], merged[:, width:]
    grad_ref[...] = jnp.where(y < 2, low, high)
    other_ref[...] = jnp.where(y < 2, high, low).astype(BF16)
    grads(CUTS[1], PIECES)

    def settle(o, carry):
        @pl.when((o > 0) & (o >= count - AHEAD))
        def _():
            xz(o).wait_send()

        @pl.when(o > 0)
        def _():
            home(o).wait_send()

        for k in range(2):
            to_core(k, o).wait_send()
            to_plane(k, o).wait_send()
        return carry

    lax.fori_loop(0, count, settle, 0)

    def settle_sums(q, carry):
        tokens_out(q).wait()
        for k in range(2):
            sum_core(k, q).wait_send()
            for i in range(parts):
                sum_plane(k, q * parts + i).wait_send()
        return carry

    lax.fori_loop(0, chunks, settle_sums, 0)
    for k in range(2):
        behind_out(k).wait()

    def settle_grads(n, carry):
        grad_out(n).wait()
        return carry

    lax.fori_loop(PIECES - SLOTS_OUT, PIECES, settle_grads, 0)


def finish_kernel(rows_hbm, behind_hbm, held_hbm, gate_hbm, up_hbm, down_hbm, turned, rows, made, load_sems, sems):
    width = rows.shape[2] // 2

    def load(k, step):
        source, target = ((rows_hbm, rows), (held_hbm, made.at[2]))[k]
        return pltpu.make_async_copy(source.at[step], target.at[step], load_sems.at[k, step])

    def outs(k, step):
        for half in range(2):
            target = (gate_hbm, up_hbm, down_hbm)[k]
            yield pltpu.make_async_copy(
                made.at[k, step, :, pl.ds(half * width, width)],
                target.at[0, :, pl.ds((step + 4 * half) * width, width)],
                sems.at[k, step, half],
            )

    first = pltpu.make_async_copy(behind_hbm, turned, load_sems.at[2, 0])
    first.start()
    for step in range(PIECES):
        for k in range(2):
            load(k, step).start()
    first.wait()
    for step in range(PIECES):
        load(1, step).wait()
        for copy in outs(2, step):
            copy.start()
        load(0, step).wait()
        for k in range(2):
            made[k, step] = nn(turned[k], rows[step]).astype(BF16)
            for copy in outs(k, step):
                copy.start()
    for k in range(3):
        for step in range(PIECES):
            for copy in outs(k, step):
                copy.wait()


def shards(tokens, cotangent, route_scale, expert_index, gate_matrix, up_matrix, down_matrix):
    rows_here, features = tokens.shape
    top = expert_index.shape[1]
    experts = lax.axis_size("aa")
    capacity = 3 * rows_here * top // (2 * experts)
    slots = experts * capacity
    width = features // 8
    wide = 2 * width
    hidden = gate_matrix.shape[2]
    group = experts // 4 if experts >= 4 else 1
    chunks = experts // group
    depth = group * capacity
    any_, vmem, dma = pl.ANY, pltpu.VMEM, pltpu.SemaphoreType.DMA
    mine, other, held, slot_rows, behind = pl.pallas_call(
        functools.partial(exchange_kernel, capacity),
        out_shape=(
            jax.ShapeDtypeStruct((rows_here, width), F32),
            jax.ShapeDtypeStruct((rows_here, width), BF16),
            jax.ShapeDtypeStruct((PIECES, hidden, wide), BF16),
            jax.ShapeDtypeStruct((PIECES, slots, wide), BF16),
            jax.ShapeDtypeStruct((2, hidden, slots), BF16),
        ),
        in_specs=[pl.BlockSpec(memory_space=vmem)] * 2 + [pl.BlockSpec(memory_space=any_)] * 5,
        out_specs=(pl.BlockSpec(memory_space=vmem), pl.BlockSpec(memory_space=vmem)) + (pl.BlockSpec(memory_space=any_),) * 3,
        scratch_shapes=[
            vmem((2, PIECES, slots, wide), BF16),
            vmem((3, PIECES, hidden, wide), BF16),
            vmem((2, rows_here, wide), BF16),
            vmem((experts, 2, capacity, wide), BF16),
            vmem((slots, rows_here), BF16),
            vmem((experts, rows_here), F32),
            vmem((experts, rows_here), F32),
            vmem((3, depth, hidden), F32),
            vmem((3, slots, hidden), BF16),
            vmem((2, slots, wide), BF16),
            vmem((2, slots, wide), BF16),
            vmem((slots, wide), BF16),
            vmem((slots, wide), F32),
            vmem((slots, wide), BF16),
            vmem((slots, wide), BF16),
            vmem((slots, wide), BF16),
            vmem((3, hidden, slots), BF16),
            vmem((SLOTS_OUT, hidden, wide), BF16),
            dma((2, 2)),
            dma((3, 2, PIECES)),
            dma((experts,)),
            dma((experts,)),
            dma((2, experts)),
            dma((2, experts)),
            dma((2, experts)),
            dma((2, experts)),
            dma((2, chunks)),
            dma((2, chunks)),
            dma((2, 2 * chunks)),
            dma((2, 2 * chunks)),
            dma((experts,)),
            dma((experts,)),
            dma((SLOTS_OUT,)),
            dma((2, chunks)),
        ],
        compiler_params=pltpu.CompilerParams(
            collective_id=0, has_side_effects=True, vmem_limit_bytes=56 * 2**20
        ),
        cost_estimate=pl.CostEstimate(
            flops=12 * slots * features * hidden,
            bytes_accessed=12 * features * hidden,
            transcendentals=slots * hidden,
        ),
    )(expert_index.T, route_scale.T, tokens, cotangent, jnp.swapaxes(gate_matrix, 1, 2), jnp.swapaxes(up_matrix, 1, 2), down_matrix)
    swapped = lax.ppermute(other, "ba", [(i, (i + 4) % 8) for i in range(8)])
    token_grad = (mine + swapped.astype(F32)).astype(BF16)
    gate_grad, up_grad, down_grad = pl.pallas_call(
        finish_kernel,
        out_shape=[jax.ShapeDtypeStruct((1, hidden, features), BF16)] * 3,
        in_specs=[pl.BlockSpec(memory_space=any_)] * 3,
        out_specs=[pl.BlockSpec(memory_space=any_)] * 3,
        scratch_shapes=[
            vmem((2, hidden, slots), BF16),
            vmem((PIECES, slots, wide), BF16),
            vmem((3, PIECES, hidden, wide), BF16),
            dma((3, PIECES)),
            dma((3, PIECES, 2)),
        ],
        compiler_params=pltpu.CompilerParams(vmem_limit_bytes=56 * 2**20),
        cost_estimate=pl.CostEstimate(
            flops=4 * slots * features * hidden,
            bytes_accessed=8 * features * hidden + 2 * slots * features,
            transcendentals=0,
        ),
    )(slot_rows, behind, held)
    return token_grad, jnp.swapaxes(gate_grad, 1, 2), jnp.swapaxes(up_grad, 1, 2), down_grad


def solution(mesh):
    in_specs = (
        P("aa", None),
        P("aa", None),
        P("aa", None),
        P("aa", None),
        P("aa", None, "ba"),
        P("aa", None, "ba"),
        P("aa", "ba", None),
    )
    out_specs = (P("aa", "ba"), P("aa", None, "ba"), P("aa", None, "ba"), P("aa", "ba", None))
    return jax.shard_map(shards, mesh=mesh, in_specs=in_specs, out_specs=out_specs, check_vma=False)
```

```python
import functools

import jax
import jax.numpy as jnp
from jax import lax
from jax.experimental import pallas as pl
from jax.experimental.pallas import tpu as pltpu
from jax.sharding import PartitionSpec as P

PIECES = 4
GRID = 4
AHEAD = 6
MOVES = (
    (0, 0), (1, 0), (3, 0), (0, 1), (0, 3), (2, 0), (0, 2), (2, 2),
    (2, 1), (2, 3), (1, 2), (3, 2), (1, 1), (3, 3), (1, 3), (3, 1),
)
RELAY_LAG = 3
SLOTS_OUT = 4
CUTS = (0, 4)
BF16 = jnp.bfloat16
F32 = jnp.float32


def nt(a, b):
    return lax.dot_general(a, b, (((1,), (1,)), ((), ())), preferred_element_type=F32)


def tn(a, b):
    return lax.dot_general(a, b, (((0,), (0,)), ((), ())), preferred_element_type=F32)


def nn(a, b):
    return jnp.dot(a, b, preferred_element_type=F32)


def shifted(me, step, count, sign):
    if count != GRID * GRID:
        return lax.rem(me + sign * step + count, count)
    move = 0
    for k, (dx, dz) in enumerate(MOVES):
        move = jnp.where(step == k, dx * GRID + dz, move)
    first, second = lax.div(move, GRID), lax.rem(move, GRID)
    row = lax.rem(lax.div(me, GRID) + sign * first + GRID, GRID)
    column = lax.rem(lax.rem(me, GRID) + sign * second + GRID, GRID)
    return row * GRID + column


def exchange_kernel(
    capacity,
    index_ref, scale_ref, tok_hbm, cot_hbm, gate_hbm, up_hbm, down_hbm,
    grad_ref, other_ref, weights_hbm, tokens_out_hbm, behind_hbm,
    rows, weights_v, piece, stage, select, rank, weight, total, act,
    to_pair, from_pair, to_y, keep, from_y, final, back, turned, made,
    piece_sem, load_sem, xz_s, xz_r, pair_s, pair_r, y_s, y_r, rp_s, rp_r, ry_s, ry_r, rx_s, rx_r,
    out_sem, pass_sem,
):
    count = lax.axis_size("aa")
    tokens = tok_hbm.shape[0]
    top = index_ref.shape[0]
    slots = count * capacity
    wide = rows.shape[3]
    width = wide // 2
    group = count // 4 if count >= 4 else 1
    chunks = count // group
    depth = group * capacity
    parts = 2 if group % 2 == 0 else 1
    me = lax.axis_index("aa")
    b = lax.axis_index("ba")
    y, c = lax.div(b, 2), lax.rem(b, 2)
    h = lax.rem(y, 2)
    own = 2 * h + c
    other = 2 * (1 - h) + c
    pair = 2 * y + 1 - c
    after = 2 * lax.rem(y + 1, 4) + c
    before = 2 * lax.rem(y + 3, 4) + c
    across = lax.rem(b + 4, 8)

    barrier = pltpu.get_barrier_semaphore()

    def greet(step, carry):
        pl.semaphore_signal(barrier, inc=1, device_id={"aa": shifted(me, step, count, 1)}, device_id_type=pl.DeviceIdType.MESH)
        return carry

    lax.fori_loop(1, count, greet, 0)
    for neighbour in (pair, after, before, across):
        pl.semaphore_signal(barrier, inc=1, device_id={"ba": neighbour}, device_id_type=pl.DeviceIdType.MESH)

    def piece_load(array, half):
        source = (tok_hbm, cot_hbm)[array]
        start = pl.multiple_of((own + 4 * half) * width, 128)
        return pltpu.make_async_copy(
            source.at[:, pl.ds(start, width)], piece.at[array, :, pl.ds(half * width, width)], piece_sem.at[array, half])

    for array in range(2):
        for half in range(2):
            piece_load(array, half).start()

    def weight_loads(p):
        made = []
        for half in range(2):
            far = (p + 4 * half) * width
            near = half * width
            for k, source in enumerate((gate_hbm, up_hbm, down_hbm)):
                made.append(pltpu.make_async_copy(source.at[0, :, pl.ds(far, width)], weights_v.at[k, p, :, pl.ds(near, width)], load_sem.at[k, half, p]))
        return made

    labels = lax.broadcasted_iota(jnp.int32, (count, tokens), 0)
    chosen = jnp.zeros((count, tokens), F32)
    scales = jnp.zeros((count, tokens), F32)
    for k in range(top):
        hit = labels == index_ref[k : k + 1, :]
        chosen = jnp.where(hit, 1.0, chosen)
        scales = jnp.where(hit, scale_ref[k : k + 1, :], scales)
    earlier = lax.broadcasted_iota(jnp.int32, (tokens, tokens), 0) < lax.broadcasted_iota(jnp.int32, (tokens, tokens), 1)
    ranks = nn(chosen.astype(BF16), jnp.where(earlier, 1.0, 0.0).astype(BF16))
    rank[...] = jnp.where(chosen > 0.5, ranks, -1.0)
    weight[...] = scales

    def remote(src, dst, send, recv, **where):
        return pltpu.make_async_remote_copy(
            src_ref=src, dst_ref=dst, send_sem=send, recv_sem=recv, device_id=where, device_id_type=pl.DeviceIdType.MESH)

    def block(o):
        return pl.ds(pl.multiple_of(o * capacity, 16), capacity)

    def chunk(q):
        return pl.ds(pl.multiple_of(q * depth, 16), depth)

    def xz(o):
        return remote(stage.at[o], rows.at[:, own, block(o), :], xz_s.at[o], xz_r.at[o], aa=shifted(me, o, count, 1))

    def to_core(k, o):
        there = rows.at[:, (own, other)[k], block(o), :]
        return remote(there, there, pair_s.at[k, o], pair_r.at[k, o], ba=pair)

    def to_plane(k, o):
        there = rows.at[:, own, block(o), pl.ds(k * width, width)]
        return remote(there, there, y_s.at[k, o], y_r.at[k, o], ba=(after, before)[k])

    def sum_core(k, q):
        return remote(to_pair.at[k, chunk(q), :], from_pair.at[k, chunk(q), :], rp_s.at[k, q], rp_r.at[k, q], ba=pair)

    def portion(i):
        return pl.ds(pl.multiple_of(i * (depth // parts), 16), depth // parts)

    def sum_plane(k, i):
        half = pl.ds(k * width, width)
        return remote(to_y.at[portion(i), half], from_y.at[portion(i), half], ry_s.at[k, i], ry_r.at[k, i], ba=(before, after)[k])

    def home(o):
        return remote(final.at[block(o), :], back.at[block(o), :], rx_s.at[o], rx_r.at[o], aa=shifted(me, o, count, -1))

    def tokens_out(q):
        return pltpu.make_async_copy(rows.at[0, :, chunk(q), :], tokens_out_hbm.at[:, chunk(q), :], pass_sem.at[0, q])

    def behind_out(k):
        return pltpu.make_async_copy(turned.at[k + 1], behind_hbm.at[k], pass_sem.at[1, k])

    def grad_out(n):
        slot = lax.rem(n, SLOTS_OUT)
        return pltpu.make_async_copy(made.at[slot], weights_hbm.at[n], out_sem.at[slot])

    def grad_step(n, carry):
        made[lax.rem(n, SLOTS_OUT)] = nn(turned[0], rows[1, n]).astype(BF16)
        grad_out(n).start()
        return carry

    def grads(first, last):
        lax.fori_loop(first, last, grad_step, 0)

    for array in range(2):
        for half in range(2):
            piece_load(array, half).wait()
    def dispatch(step, carry):
        o = lax.rem(step + 1, count)
        expert = shifted(me, o, count, 1)
        hits = rank[pl.ds(expert, 1), :] == lax.broadcasted_iota(jnp.int32, (capacity, tokens), 0).astype(F32)
        picks = jnp.where(hits, 1.0, 0.0)
        scale = jnp.sum(picks * weight[pl.ds(expert, 1), :], axis=1, keepdims=True)
        picks = picks.astype(BF16)
        select[block(o), :] = picks
        stage[o, 0] = nn(picks, piece[0]).astype(BF16)
        stage[o, 1] = (scale * nn(picks, piece[1])).astype(BF16)

        return carry

    def first_sends(o, carry):
        xz(o).start()
        return carry

    ahead = min(AHEAD, count)
    lax.fori_loop(0, ahead - 1, dispatch, 0)
    pl.semaphore_wait(barrier, count - 1 + 4)
    lax.fori_loop(1, ahead, first_sends, 0)
    lax.fori_loop(ahead - 1, count, dispatch, 0)
    for a in range(2):
        rows[a, own, 0:capacity, :] = stage[0, a]
    for p in range(PIECES):
        for load in weight_loads(p):
            load.start()

    lag_c = group + RELAY_LAG + 1
    lag_d = lag_c + 3
    lag_e = lag_d + 5
    steps = lag_d + 4 * chunks - 2

    def send_home(n):
        sum_plane(0, n).wait_recv()
        sum_plane(1, n).wait_recv()
        final[portion(n), :] = (keep[portion(n), :] + from_y[portion(n), :].astype(F32)).astype(BF16)
        for i in range(group // parts):
            o = n * (group // parts) + i

            @pl.when(o > 0)
            def _():
                home(o).start()

            @pl.when(o == 0)
            def _():
                back[0:capacity, :] = final[0:capacity, :]

    def backward_unit(w, carry):
        q, j = lax.div(w, 4), lax.rem(w, 4)
        plane = jnp.where(lax.rem(j, 2) == 0, 1 - h, h)
        core = jnp.where(j < 2, 1 - c, c)
        p = 2 * plane + core
        part = nn(act[1, chunk(q), :], weights_v[0, p]) + nn(act[2, chunk(q), :], weights_v[1, p])

        @pl.when(j < 2)
        def _():
            to_pair[j, chunk(q), :] = part.astype(BF16)
            sum_core(j, q).start()

        @pl.when(j == 2)
        def _():
            sum_core(0, q).wait_recv()
            to_y[chunk(q), :] = (part + from_pair[0, chunk(q), :].astype(F32)).astype(BF16)
            for i in range(parts):
                sum_plane(0, q * parts + i).start()
                sum_plane(1, q * parts + i).start()

        @pl.when(j == 3)
        def _():
            sum_core(1, q).wait_recv()
            keep[chunk(q), :] = part + from_pair[1, chunk(q), :].astype(F32)
        return carry

    def main(t, carry):
        @pl.when(t < count)
        def _():
            @pl.when(t > 0)
            def _():
                xz(t).wait_recv()

            to_plane(0, t).start()
            to_plane(1, t).start()
            to_core(0, t).start()

            @pl.when(t + AHEAD < count)
            def _():
                @pl.when(t > 0)
                def _():
                    xz(t).wait_send()

                xz(t + AHEAD).start()

        u = t - RELAY_LAG

        @pl.when((u >= 0) & (u < count))
        def _():
            to_plane(0, u).wait_recv()
            to_plane(1, u).wait_recv()
            to_core(1, u).start()

        v = t - lag_c

        @pl.when((v >= 0) & (v < 4 * chunks))
        def _():
            q, j = lax.div(v, 4), lax.rem(v, 4)

            @pl.when(v == 0)
            def _():
                for p in range(PIECES):
                    for load in weight_loads(p):
                        load.wait()

            @pl.when(j == 0)
            def _():
                for i in range(group):
                    to_core(0, q * group + i).wait_recv()
                    to_core(1, q * group + i).wait_recv()
                tokens_out(q).start()

            @pl.when(j < 3)
            def _():
                side = jnp.where(j == 2, 1, 0)
                total[j] = sum(nt(rows[side, p, chunk(q), :], weights_v[j, p]) for p in range(PIECES))

            @pl.when(j == 2)
            def _():
                gate, up, behind = total[0], total[1], total[2]
                sigmoid = jax.nn.sigmoid(gate)
                active = gate * sigmoid
                act[0, chunk(q), :] = (active * up).astype(BF16)
                act[1, chunk(q), :] = (behind * up * sigmoid * (1.0 + gate * (1.0 - sigmoid))).astype(BF16)
                act[2, chunk(q), :] = (behind * active).astype(BF16)

        w = t - lag_d

        @pl.when((w >= 0) & (w < 4 * chunks - 2))
        def _():
            backward_unit(w, 0)

        z = t - lag_e

        @pl.when((z >= 0) & (z < 4 * (chunks - 1)) & (lax.rem(z + 4, 4) == 0))
        def _():
            for i in range(parts):
                send_home(lax.div(z, 4) * parts + i)

        return carry

    lax.fori_loop(0, steps, main, 0)

    turned[0] = act[0].T
    lax.fori_loop(4 * chunks - 2, 4 * chunks, backward_unit, 0)
    for k in range(2):
        turned[k + 1] = act[k + 1].T
        behind_out(k).start()
    grads(0, CUTS[0])
    for i in range(parts):
        send_home(jnp.int32((chunks - 1) * parts + i))
        grads(CUTS[0] + i, CUTS[0] + i + 1)
    grads(CUTS[0] + parts, CUTS[1])

    def arrive(o, carry):
        home(o).wait_recv()
        return carry

    early = (chunks - 1) * depth
    lax.fori_loop(1, count - group, arrive, 0)
    keep[0:tokens, :] = tn(select[0:early, :], back[0:early, :])
    lax.fori_loop(count - group, count, arrive, 0)
    merged = keep[0:tokens, :] + tn(select[early:slots, :], back[early:slots, :])
    low, high = merged[:, :width], merged[:, width:]
    grad_ref[...] = jnp.where(y < 2, low, high)
    other_ref[...] = jnp.where(y < 2, high, low).astype(BF16)
    grads(CUTS[1], PIECES)

    def settle(o, carry):
        @pl.when((o > 0) & (o >= count - AHEAD))
        def _():
            xz(o).wait_send()

        @pl.when(o > 0)
        def _():
            home(o).wait_send()

        for k in range(2):
            to_core(k, o).wait_send()
            to_plane(k, o).wait_send()
        return carry

    lax.fori_loop(0, count, settle, 0)

    def settle_sums(q, carry):
        tokens_out(q).wait()
        for k in range(2):
            sum_core(k, q).wait_send()
            for i in range(parts):
                sum_plane(k, q * parts + i).wait_send()
        return carry

    lax.fori_loop(0, chunks, settle_sums, 0)
    for k in range(2):
        behind_out(k).wait()

    def settle_grads(n, carry):
        grad_out(n).wait()
        return carry

    lax.fori_loop(PIECES - SLOTS_OUT, PIECES, settle_grads, 0)


def finish_kernel(rows_hbm, behind_hbm, held_hbm, gate_hbm, up_hbm, down_hbm, turned, rows, made, load_sems, sems):
    width = rows.shape[2] // 2

    def load(k, step):
        source, target = ((rows_hbm, rows), (held_hbm, made.at[2]))[k]
        return pltpu.make_async_copy(source.at[step], target.at[step], load_sems.at[k, step])

    def outs(k, step):
        for half in range(2):
            target = (gate_hbm, up_hbm, down_hbm)[k]
            yield pltpu.make_async_copy(
                made.at[k, step, :, pl.ds(half * width, width)],
                target.at[0, :, pl.ds((step + 4 * half) * width, width)],
                sems.at[k, step, half],
            )

    first = pltpu.make_async_copy(behind_hbm, turned, load_sems.at[2, 0])
    first.start()
    for step in range(PIECES):
        for k in range(2):
            load(k, step).start()
    first.wait()
    for step in range(PIECES):
        load(1, step).wait()
        for copy in outs(2, step):
            copy.start()
        load(0, step).wait()
        for k in range(2):
            made[k, step] = nn(turned[k], rows[step]).astype(BF16)
            for copy in outs(k, step):
                copy.start()
    for k in range(3):
        for step in range(PIECES):
            for copy in outs(k, step):
                copy.wait()


def shards(tokens, cotangent, route_scale, expert_index, gate_matrix, up_matrix, down_matrix):
    rows_here, features = tokens.shape
    top = expert_index.shape[1]
    experts = lax.axis_size("aa")
    capacity = 3 * rows_here * top // (2 * experts)
    slots = experts * capacity
    width = features // 8
    wide = 2 * width
    hidden = gate_matrix.shape[2]
    group = experts // 4 if experts >= 4 else 1
    chunks = experts // group
    depth = group * capacity
    any_, vmem, dma = pl.ANY, pltpu.VMEM, pltpu.SemaphoreType.DMA
    mine, other, held, slot_rows, behind = pl.pallas_call(
        functools.partial(exchange_kernel, capacity),
        out_shape=(
            jax.ShapeDtypeStruct((rows_here, width), F32),
            jax.ShapeDtypeStruct((rows_here, width), BF16),
            jax.ShapeDtypeStruct((PIECES, hidden, wide), BF16),
            jax.ShapeDtypeStruct((PIECES, slots, wide), BF16),
            jax.ShapeDtypeStruct((2, hidden, slots), BF16),
        ),
        in_specs=[pl.BlockSpec(memory_space=vmem)] * 2 + [pl.BlockSpec(memory_space=any_)] * 5,
        out_specs=(pl.BlockSpec(memory_space=vmem), pl.BlockSpec(memory_space=vmem)) + (pl.BlockSpec(memory_space=any_),) * 3,
        scratch_shapes=[
            vmem((2, PIECES, slots, wide), BF16),
            vmem((3, PIECES, hidden, wide), BF16),
            vmem((2, rows_here, wide), BF16),
            vmem((experts, 2, capacity, wide), BF16),
            vmem((slots, rows_here), BF16),
            vmem((experts, rows_here), F32),
            vmem((experts, rows_here), F32),
            vmem((3, depth, hidden), F32),
            vmem((3, slots, hidden), BF16),
            vmem((2, slots, wide), BF16),
            vmem((2, slots, wide), BF16),
            vmem((slots, wide), BF16),
            vmem((slots, wide), F32),
            vmem((slots, wide), BF16),
            vmem((slots, wide), BF16),
            vmem((slots, wide), BF16),
            vmem((3, hidden, slots), BF16),
            vmem((SLOTS_OUT, hidden, wide), BF16),
            dma((2, 2)),
            dma((3, 2, PIECES)),
            dma((experts,)),
            dma((experts,)),
            dma((2, experts)),
            dma((2, experts)),
            dma((2, experts)),
            dma((2, experts)),
            dma((2, chunks)),
            dma((2, chunks)),
            dma((2, 2 * chunks)),
            dma((2, 2 * chunks)),
            dma((experts,)),
            dma((experts,)),
            dma((SLOTS_OUT,)),
            dma((2, chunks)),
        ],
        compiler_params=pltpu.CompilerParams(
            collective_id=0, has_side_effects=True, vmem_limit_bytes=56 * 2**20
        ),
        cost_estimate=pl.CostEstimate(
            flops=12 * slots * features * hidden,
            bytes_accessed=12 * features * hidden,
            transcendentals=slots * hidden,
        ),
    )(expert_index.T, route_scale.T, tokens, cotangent, jnp.swapaxes(gate_matrix, 1, 2), jnp.swapaxes(up_matrix, 1, 2), down_matrix)
    swapped = lax.ppermute(other, "ba", [(i, (i + 4) % 8) for i in range(8)])
    token_grad = (mine + swapped.astype(F32)).astype(BF16)
    gate_grad, up_grad, down_grad = pl.pallas_call(
        finish_kernel,
        out_shape=[jax.ShapeDtypeStruct((1, hidden, features), BF16)] * 3,
        in_specs=[pl.BlockSpec(memory_space=any_)] * 3,
        out_specs=[pl.BlockSpec(memory_space=any_)] * 3,
        scratch_shapes=[
            vmem((2, hidden, slots), BF16),
            vmem((PIECES, slots, wide), BF16),
            vmem((3, PIECES, hidden, wide), BF16),
            dma((3, PIECES)),
            dma((3, PIECES, 2)),
        ],
        compiler_params=pltpu.CompilerParams(vmem_limit_bytes=56 * 2**20),
        cost_estimate=pl.CostEstimate(
            flops=4 * slots * features * hidden,
            bytes_accessed=8 * features * hidden + 2 * slots * features,
            transcendentals=0,
        ),
    )(slot_rows, behind, held)
    return token_grad, jnp.swapaxes(gate_grad, 1, 2), jnp.swapaxes(up_grad, 1, 2), down_grad


def solution(mesh):
    in_specs = (
        P("aa", None),
        P("aa", None),
        P("aa", None),
        P("aa", None),
        P("aa", None, "ba"),
        P("aa", None, "ba"),
        P("aa", "ba", None),
    )
    out_specs = (P("aa", "ba"), P("aa", None, "ba"), P("aa", None, "ba"), P("aa", "ba", None))
    return jax.shard_map(shards, mesh=mesh, in_specs=in_specs, out_specs=out_specs, check_vma=False)
```
